32 devices in a mesh: box: 8 (over y, x, core), grp: 4 (over z).
Axes of the slice: x: 2, y: 2, z: 4, core: 2. Of those that a mesh axis runs over, the one named last changes fastest.
Arguments:
- impedance: bfloat16 [2, 8, 1, 2048, 2048], P(None, 'box', None, None, 'grp'), may hold values from -3 to 3
- face_order: int32 [8, 1, 16], replicated, may hold values from 0 to 15, each once within a row
Outputs:
- merged: bfloat16 [2, 8, 1, 4096, 2048], P(None, 'box', None, None, 'grp')
The draws below stay inside these ranges and needn't reach their ends.
Inputs may be any that keep to these rules, and one draw needn't show every extreme that they name: `face_order`: each row lists the 16 face blocks of one box once; its first 3 entries are the blocks on the face shared with the sibling, the k-th facing the sibling's k-th.
All inputs are finite; a program needn't handle non-finite values.
Results may differ from the reference program's by a relative error of at most 0.0035.
Values may be sent and summed in bfloat16 or wider, within the bound.
A program may use at most 64 MiB of HBM per device.

```python
import jax
import jax.numpy as jnp
from jax import lax

NB = 2048
BLK = 128
FB = 16
MB = 3
NS_STEPS = 2
BOX_DEV = 1
GROUPS = 8


def draw_impedance(key, part):
    full_shape = (2, GROUPS, BOX_DEV, NB, NB)
    entries = jax.random.truncated_normal(key, -3.0, 3.0, full_shape, jnp.float32)
    return entries.astype(jnp.bfloat16)


def setup_inputs(seed: int = 0) -> dict:
    arg_keys = jax.random.split(jax.random.key(seed), 3)
    impedance = draw_impedance(jax.random.fold_in(arg_keys[2], 71), 0)
    face_order = jax.vmap(lambda own: jax.random.permutation(own, FB))(jax.random.split(arg_keys[1], GROUPS * BOX_DEV)).reshape((GROUPS, BOX_DEV, FB)).astype(jnp.int32)
    return {"impedance": impedance, "face_order": face_order}


HIGHEST_PREC = lax.Precision.HIGHEST


def complex_dot(left_mat, right_mat, precision):
    real_part = jnp.dot(left_mat[0], right_mat[0], precision=precision, preferred_element_type=jnp.float32) - jnp.dot(left_mat[1], right_mat[1], precision=precision, preferred_element_type=jnp.float32)
    imag_part = jnp.dot(left_mat[0], right_mat[1], precision=precision, preferred_element_type=jnp.float32) + jnp.dot(left_mat[1], right_mat[0], precision=precision, preferred_element_type=jnp.float32)
    return jnp.stack([real_part, imag_part])


def iface_index(face_list):
    return (face_list[:MB, None] * BLK + jnp.arange(BLK, dtype=jnp.int32)[None, :]).reshape(MB * BLK).astype(jnp.int32)


def exterior_mask(face_list):
    block_ids = jnp.arange(NB, dtype=jnp.int32) // BLK
    on_face = jnp.any(block_ids[:, None] == face_list[None, :MB], axis=1)
    return jnp.where(on_face, jnp.float32(0.0), jnp.float32(1.0)).astype(jnp.float32)


def merge_pair(pair_item):
    box_maps, orders = pair_item
    coupling_sq = 1.0 / NB
    coupling = NB ** -0.5
    iface_len = MB * BLK
    identity = jnp.eye(iface_len, dtype=jnp.float32)
    ident_pair = jnp.stack([identity, jnp.zeros_like(identity)])
    point_lists = [iface_index(orders[0]), iface_index(orders[1])]
    ext_masks = [exterior_mask(orders[0]), exterior_mask(orders[1])]
    iface_cols = [box_maps[0][:, :, point_lists[0]], box_maps[1][:, :, point_lists[1]]]
    blocks = [iface_cols[0][:, point_lists[0], :], iface_cols[1][:, point_lists[1], :]]
    iface_rows = [box_maps[0][:, point_lists[0], :], box_maps[1][:, point_lists[1], :]]
    results = []
    for side_idx in range(2):
        twin_idx = 1 - side_idx
        coupled = complex_dot(blocks[side_idx].astype(jnp.float32), blocks[twin_idx].astype(jnp.float32), HIGHEST_PREC)
        system = ident_pair - coupling_sq * coupled
        inverse = ident_pair
        for iteration in range(NS_STEPS):
            inverse = 2.0 * inverse - complex_dot(complex_dot(inverse, system, HIGHEST_PREC), inverse, HIGHEST_PREC)
        incoming = iface_rows[side_idx].astype(jnp.float32) * ext_masks[side_idx][None, None, :]
        response = complex_dot(inverse, incoming, HIGHEST_PREC)
        echoed = complex_dot(blocks[twin_idx].astype(jnp.float32), response, HIGHEST_PREC)
        own_out = box_maps[side_idx].astype(jnp.float32) * ext_masks[side_idx][None, None, :] + coupling_sq * complex_dot(iface_cols[side_idx], echoed.astype(jnp.bfloat16), None)
        cross_out = -coupling * complex_dot(iface_cols[twin_idx], response.astype(jnp.bfloat16), None)
        if side_idx == 0:
            column = jnp.concatenate([own_out, cross_out], axis=1)
        else:
            column = jnp.concatenate([cross_out, own_out], axis=1)
        results.append(column.astype(jnp.bfloat16))
    return jnp.stack(results)


def reference(impedance, face_order):
    pair_count = GROUPS // 2
    box_maps = impedance.reshape(2, pair_count, 2, BOX_DEV, NB, NB).transpose(1, 3, 2, 0, 4, 5).reshape(pair_count * BOX_DEV, 2, 2, NB, NB)
    orders = face_order.reshape(pair_count, 2, BOX_DEV, FB).transpose(0, 2, 1, 3).reshape(pair_count * BOX_DEV, 2, FB)
    merged = lax.map(merge_pair, (box_maps, orders))
    merged = merged.reshape(pair_count, BOX_DEV, 2, 2, 2 * NB, NB).transpose(3, 0, 2, 1, 4, 5)
    return merged.reshape(2, GROUPS, BOX_DEV, 2 * NB, NB)
```

```python
import functools

import jax
import jax.numpy as jnp
from jax import lax
from jax.experimental import pallas as pl
from jax.experimental.pallas import tpu as pltpu
from jax.sharding import PartitionSpec as P

BLK = 128
MB = 3
NS_STEPS = 2
ROWS = 64
LAG = 2
MESH_ID = pl.DeviceIdType.MESH
BF16 = jnp.bfloat16
F32 = jnp.float32


def pick_kernel(order_ref, own_ref, mine_ref):
    base = lax.axis_index("box") * (own_ref.shape[1] // BLK)
    blocks = own_ref.shape[2] // BLK
    first = lax.axis_index("grp") * blocks

    def body(block, carry):
        row = pl.multiple_of(order_ref[base + block] * BLK, BLK)
        for k in range(MB):
            local = order_ref[base + k] - first
            held = jnp.logical_and(local >= 0, local < blocks).astype(F32).astype(BF16)
            col = pl.multiple_of(jnp.clip(local, 0, blocks - 1) * BLK, BLK)
            for part in range(2):
                piece = own_ref[part, pl.ds(row, BLK), pl.ds(col, BLK)]
                mine_ref[pl.ds(block * BLK, BLK), pl.ds((part * MB + k) * BLK, BLK)] = piece * held
        return carry

    lax.fori_loop(0, own_ref.shape[1] // BLK, body, 0)


def gather_kernel(
    n, mine_ref, zb_ref, zs_ref, buf_l, buf_r, out_r, out_l,
    send_r, recv_l, send_l, recv_r, send_t, recv_t,
):
    box = lax.axis_index("box")
    grp = lax.axis_index("grp")
    twin = box + 1 - 2 * lax.rem(box, 2)
    chunks = buf_l.shape[0]
    has_left = grp > 0
    has_right = grp < n - 1

    barrier = pltpu.get_barrier_semaphore()
    pl.semaphore_signal(barrier, inc=1, device_id={"box": twin}, device_id_type=MESH_ID)

    @pl.when(has_left)
    def _():
        pl.semaphore_signal(barrier, inc=1, device_id={"grp": grp - 1}, device_id_type=MESH_ID)

    @pl.when(has_right)
    def _():
        pl.semaphore_signal(barrier, inc=1, device_id={"grp": grp + 1}, device_id_type=MESH_ID)

    pl.semaphore_wait(barrier, 1 + has_left.astype(jnp.int32) + has_right.astype(jnp.int32))

    def to_right(c):
        return pltpu.make_async_remote_copy(
            src_ref=out_r.at[c], dst_ref=buf_l.at[c], send_sem=send_r.at[c], recv_sem=recv_l.at[c],
            device_id={"grp": grp + 1}, device_id_type=MESH_ID,
        )

    def to_left(c):
        return pltpu.make_async_remote_copy(
            src_ref=out_l.at[c], dst_ref=buf_r.at[c], send_sem=send_l.at[c], recv_sem=recv_r.at[c],
            device_id={"grp": grp - 1}, device_id_type=MESH_ID,
        )

    def to_twin(c):
        rows = pl.ds(c * ROWS, ROWS)
        return pltpu.make_async_remote_copy(
            src_ref=zb_ref.at[rows], dst_ref=zs_ref.at[rows], send_sem=send_t.at[c], recv_sem=recv_t.at[c],
            device_id={"box": twin}, device_id_type=MESH_ID,
        )

    def mine(c):
        return mine_ref[pl.ds(pl.multiple_of(c * ROWS, ROWS), ROWS), :]

    def left_step(c):
        @pl.when(has_left)
        def _():
            to_right(c).wait_recv()

        @pl.when(jnp.logical_not(has_left))
        def _():
            buf_l[c] = jnp.zeros(buf_l.shape[1:], BF16)

        out_r[c] = mine(c) + buf_l[c]

        @pl.when(has_right)
        def _():
            to_right(c).start()

    def right_step(c):
        @pl.when(has_right)
        def _():
            to_left(c).wait_recv()

        @pl.when(jnp.logical_not(has_right))
        def _():
            buf_r[c] = jnp.zeros(buf_r.shape[1:], BF16)

        out_l[c] = mine(c) + buf_r[c]

        @pl.when(has_left)
        def _():
            to_left(c).start()

    def full_step(c):
        zb_ref[pl.ds(c * ROWS, ROWS), :] = out_r[c] + buf_r[c]
        to_twin(c).start()

    lag_l = LAG * grp
    lag_r = LAG * (n - 1 - grp)
    lag_f = jnp.maximum(lag_l, lag_r)

    def tick(t, carry):
        for lag, step in ((lag_l, left_step), (lag_r, right_step), (lag_f, full_step)):
            c = t - lag

            @pl.when(jnp.logical_and(c >= 0, c < chunks))
            def _():
                step(c)

        return carry

    lax.fori_loop(0, chunks + LAG * (n - 1), tick, 0)

    def drain(c, carry):
        @pl.when(has_right)
        def _():
            to_right(c).wait_send()

        @pl.when(has_left)
        def _():
            to_left(c).wait_send()

        to_twin(c).wait_send()
        to_twin(c).wait_recv()
        return carry

    lax.fori_loop(0, chunks, drain, 0)


def as_right_operand(pair):
    real, imag = pair
    return jnp.concatenate(
        [jnp.concatenate([real, imag], axis=1), jnp.concatenate([-imag, real], axis=1)], axis=0
    )


def product_kernel(rows, order_ref, own_ref, zb_ref, zs_ref, ext_ref, out_ref, rhs, lo, base, held, sems):
    box = lax.axis_index("box")
    parity = lax.rem(box, 2)
    twin = box + 1 - 2 * parity
    points, width = own_ref.shape[1], own_ref.shape[2]
    face_blocks = points // BLK
    iface = MB * BLK
    coupling_sq = 1.0 / points
    coupling = points ** (-0.5)
    ext = ext_ref[...]

    def put(dst, pair):
        real, imag = pair
        dst[pl.ds(0, iface), pl.ds(0, width)] = real
        dst[pl.ds(0, iface), pl.ds(width, width)] = imag
        dst[pl.ds(iface, iface), pl.ds(0, width)] = -imag
        dst[pl.ds(iface, iface), pl.ds(width, width)] = real

    def split(value):
        high = value.astype(BF16)
        low = (value - high.astype(F32)).astype(BF16)
        put(rhs.at[0], (high[:, :width], high[:, width:]))
        put(lo, (low[:, :width], low[:, width:]))

    def apply(z_ref):
        left = z_ref[pl.ds(0, iface), :]
        return jnp.dot(left, rhs[0], preferred_element_type=F32) + jnp.dot(
            left, lo[...], preferred_element_type=F32
        )

    for k in range(MB):
        row = pl.multiple_of(order_ref[box * face_blocks + k] * BLK, BLK)
        for part in range(2):
            base[pl.ds(k * BLK, BLK), pl.ds(part * width, width)] = (
                own_ref[part, pl.ds(row, BLK), :].astype(F32) * ext
            )
    split(base[...])
    response = None
    for _ in range(2**NS_STEPS - 1):
        split(apply(zs_ref))
        response = base[...] + coupling_sq * apply(zb_ref)
        split(response)
    echoed = apply(zs_ref).astype(BF16)
    response = response.astype(BF16)
    put(rhs.at[0], (echoed[:, :width], echoed[:, width:]))
    put(rhs.at[1], (response[:, :width], response[:, width:]))

    per_step = rows // BLK
    steps = points // rows

    def copy_out(slot, half, order_base, block):
        row = half * points + order_ref[order_base + block] * BLK
        return pltpu.make_async_copy(
            held.at[slot], out_ref.at[:, pl.ds(pl.multiple_of(row, BLK), BLK), :], sems.at[slot]
        )

    def own_step(s, carry):
        left = zb_ref[pl.ds(pl.multiple_of(s * rows, rows), rows), :]
        prod = coupling_sq * jnp.dot(left, rhs[0], preferred_element_type=F32)
        for j in range(per_step):
            block = s * per_step + j
            row = pl.multiple_of(order_ref[box * face_blocks + block] * BLK, BLK)
            for part in range(2):
                piece = prod[j * BLK : (j + 1) * BLK, part * width : (part + 1) * width]
                held[block, part] = (
                    own_ref[part, pl.ds(row, BLK), :].astype(F32) * ext + piece
                ).astype(BF16)
            copy_out(block, parity, box * face_blocks, block).start()
        return carry

    def cross_step(s, carry):
        left = zs_ref[pl.ds(pl.multiple_of(s * rows, rows), rows), :]
        prod = -coupling * jnp.dot(left, rhs[1], preferred_element_type=F32)
        for j in range(per_step):
            block = s * per_step + j
            for part in range(2):
                piece = prod[j * BLK : (j + 1) * BLK, part * width : (part + 1) * width]
                held[face_blocks + block, part] = piece.astype(BF16)
            copy_out(face_blocks + block, 1 - parity, twin * face_blocks, block).start()
        return carry

    lax.fori_loop(0, steps, own_step, 0)
    lax.fori_loop(0, steps, cross_step, 0)

    def drain(block, carry):
        copy_out(block, parity, box * face_blocks, block).wait()
        copy_out(face_blocks + block, 1 - parity, twin * face_blocks, block).wait()
        return carry

    lax.fori_loop(0, face_blocks, drain, 0)


def shards(impedance, face_order):
    points, width = impedance.shape[3], impedance.shape[4]
    own = impedance.reshape(2, points, width)
    order = face_order.reshape(-1)
    face_blocks = points // BLK
    iface = MB * BLK
    n = lax.axis_size("grp")
    chunks = points // ROWS
    smem = pl.BlockSpec(memory_space=pltpu.SMEM)
    vmem = pl.BlockSpec(memory_space=pltpu.VMEM)
    z_shape = jax.ShapeDtypeStruct((points, 2 * iface), BF16)
    buffer = pltpu.VMEM((chunks, ROWS, 2 * iface), BF16)
    mine = pl.pallas_call(
        pick_kernel,
        out_shape=z_shape,
        in_specs=[smem, vmem],
        out_specs=vmem,
        compiler_params=pltpu.CompilerParams(vmem_limit_bytes=16 << 20),
    )(order, own)
    z_own, z_twin = pl.pallas_call(
        functools.partial(gather_kernel, n),
        out_shape=(z_shape, z_shape),
        in_specs=[vmem],
        out_specs=(vmem, vmem),
        scratch_shapes=[buffer] * 4 + [pltpu.SemaphoreType.DMA((chunks,))] * 6,
        compiler_params=pltpu.CompilerParams(
            collective_id=0, has_side_effects=True, vmem_limit_bytes=40 << 20
        ),
    )(mine)

    box = lax.axis_index("box")
    own_order = lax.dynamic_slice_in_dim(order, box * face_blocks, MB)
    col_blocks = (lax.axis_index("grp") * width + jnp.arange(width, dtype=jnp.int32)) // BLK
    on_face = jnp.any(col_blocks[None, :] == own_order[:, None], axis=0)
    ext = jnp.where(on_face, 0.0, 1.0).astype(F32)[None, :]

    rows = 4 * BLK
    merged = pl.pallas_call(
        functools.partial(product_kernel, rows),
        out_shape=jax.ShapeDtypeStruct((2, 2 * points, width), BF16),
        in_specs=[smem, vmem, vmem, vmem, vmem],
        out_specs=pl.BlockSpec(memory_space=pl.ANY),
        scratch_shapes=[
            pltpu.VMEM((2, 2 * iface, 2 * width), BF16),
            pltpu.VMEM((2 * iface, 2 * width), BF16),
            pltpu.VMEM((iface, 2 * width), F32),
            pltpu.VMEM((2 * face_blocks, 2, BLK, width), BF16),
            pltpu.SemaphoreType.DMA((2 * face_blocks,)),
        ],
        compiler_params=pltpu.CompilerParams(vmem_limit_bytes=48 << 20),
    )(order, own, z_own, z_twin, ext)
    return merged[:, None, None]


def solution(mesh):
    in_specs = (P(None, "box", None, None, "grp"), P())
    out_specs = P(None, "box", None, None, "grp")
    return jax.shard_map(shards, mesh=mesh, in_specs=in_specs, out_specs=out_specs, check_vma=False)
```

```python
import functools

import jax
import jax.numpy as jnp
from jax import lax
from jax.experimental import pallas as pl
from jax.experimental.pallas import tpu as pltpu
from jax.sharding import PartitionSpec as P

BLK = 128
MB = 3
NS_STEPS = 2
ROWS = 64
LAG = 2
MESH_ID = pl.DeviceIdType.MESH
BF16 = jnp.bfloat16
F32 = jnp.float32


def exterior(order_ref, base, width):
    blocks = width // BLK
    first = lax.axis_index("grp") * blocks
    pieces = []
    for j in range(blocks):
        keep = order_ref[base] != first + j
        for k in range(1, MB):
            keep = jnp.logical_and(keep, order_ref[base + k] != first + j)
        pieces.append(jnp.full((1, BLK), keep.astype(F32), F32))
    return jnp.concatenate(pieces, axis=1)


def pick_kernel(order_ref, own_ref, mine_ref, rows_ref):
    width = own_ref.shape[2]
    base = lax.axis_index("box") * (own_ref.shape[1] // BLK)
    blocks = width // BLK
    first = lax.axis_index("grp") * blocks
    ext = exterior(order_ref, base, width)
    for k in range(MB):
        row = pl.multiple_of(order_ref[base + k] * BLK, BLK)
        for part in range(2):
            rows_ref[pl.ds(k * BLK, BLK), pl.ds(part * width, width)] = (
                own_ref[part, pl.ds(row, BLK), :].astype(F32) * ext
            ).astype(BF16)

    def body(block, carry):
        row = pl.multiple_of(order_ref[base + block] * BLK, BLK)
        for k in range(MB):
            local = order_ref[base + k] - first
            held = jnp.logical_and(local >= 0, local < blocks).astype(F32).astype(BF16)
            col = pl.multiple_of(jnp.clip(local, 0, blocks - 1) * BLK, BLK)
            for part in range(2):
                piece = own_ref[part, pl.ds(row, BLK), pl.ds(col, BLK)]
                mine_ref[pl.ds(block * BLK, BLK), pl.ds((part * MB + k) * BLK, BLK)] = piece * held
        return carry

    lax.fori_loop(0, own_ref.shape[1] // BLK, body, 0)


def put(dst, real, imag):
    depth, width = real.shape
    dst[pl.ds(0, depth), pl.ds(0, width)] = real
    dst[pl.ds(0, depth), pl.ds(width, width)] = imag
    dst[pl.ds(depth, depth), pl.ds(0, width)] = -imag
    dst[pl.ds(depth, depth), pl.ds(width, width)] = real


def gather_kernel(
    n, mine_ref, rows_ref, zb_ref, zs_ref, rhs_ref, high, low, buf_l, buf_r, out_r, out_l,
    send_r, recv_l, send_l, recv_r, send_t, recv_t,
):
    box = lax.axis_index("box")
    grp = lax.axis_index("grp")
    twin = box + 1 - 2 * lax.rem(box, 2)
    chunks = buf_l.shape[0]
    has_left = grp > 0
    has_right = grp < n - 1

    barrier = pltpu.get_barrier_semaphore()
    pl.semaphore_signal(barrier, inc=1, device_id={"box": twin}, device_id_type=MESH_ID)

    @pl.when(has_left)
    def _():
        pl.semaphore_signal(barrier, inc=1, device_id={"grp": grp - 1}, device_id_type=MESH_ID)

    @pl.when(has_right)
    def _():
        pl.semaphore_signal(barrier, inc=1, device_id={"grp": grp + 1}, device_id_type=MESH_ID)

    pl.semaphore_wait(barrier, 1 + has_left.astype(jnp.int32) + has_right.astype(jnp.int32))

    def to_right(c):
        return pltpu.make_async_remote_copy(
            src_ref=out_r.at[c], dst_ref=buf_l.at[c], send_sem=send_r.at[c], recv_sem=recv_l.at[c],
            device_id={"grp": grp + 1}, device_id_type=MESH_ID,
        )

    def to_left(c):
        return pltpu.make_async_remote_copy(
            src_ref=out_l.at[c], dst_ref=buf_r.at[c], send_sem=send_l.at[c], recv_sem=recv_r.at[c],
            device_id={"grp": grp - 1}, device_id_type=MESH_ID,
        )

    def to_twin(c):
        rows = pl.ds(c * ROWS, ROWS)
        return pltpu.make_async_remote_copy(
            src_ref=zb_ref.at[rows], dst_ref=zs_ref.at[rows], send_sem=send_t.at[c], recv_sem=recv_t.at[c],
            device_id={"box": twin}, device_id_type=MESH_ID,
        )

    def mine(c):
        return mine_ref[pl.ds(pl.multiple_of(c * ROWS, ROWS), ROWS), :]

    def left_step(c):
        @pl.when(has_left)
        def _():
            to_right(c).wait_recv()

        @pl.when(jnp.logical_not(has_left))
        def _():
            buf_l[c] = jnp.zeros(buf_l.shape[1:], BF16)

        out_r[c] = mine(c) + buf_l[c]

        @pl.when(has_right)
        def _():
            to_right(c).start()

    def right_step(c):
        @pl.when(has_right)
        def _():
            to_left(c).wait_recv()

        @pl.when(jnp.logical_not(has_right))
        def _():
            buf_r[c] = jnp.zeros(buf_r.shape[1:], BF16)

        out_l[c] = mine(c) + buf_r[c]

        @pl.when(has_left)
        def _():
            to_left(c).start()

    def full_step(c):
        zb_ref[pl.ds(c * ROWS, ROWS), :] = out_r[c] + buf_r[c]
        to_twin(c).start()

    points, width = zb_ref.shape[0], rows_ref.shape[1] // 2
    coupling_sq = 1.0 / points
    iface = MB * BLK

    def split(value):
        top = value.astype(BF16)
        rest = (value - top.astype(F32)).astype(BF16)
        put(high, top[:, :width], top[:, width:])
        put(low, rest[:, :width], rest[:, width:])

    def apply(z_ref):
        left = z_ref[pl.ds(0, iface), :]
        return jnp.dot(left, high[...], preferred_element_type=F32) + jnp.dot(
            left, low[...], preferred_element_type=F32
        )

    face_chunks = iface // ROWS
    stages = 2 * (2**NS_STEPS - 1)

    def response_stage(stage):
        if stage == 0:
            for c in range(face_chunks):
                to_twin(c).wait_recv()
            put(high, rows_ref[:, :width], rows_ref[:, width:])
            split(jnp.dot(zs_ref[pl.ds(0, iface), :], high[...], preferred_element_type=F32))
        elif stage == stages:
            rhs_ref[1] = high[...]
            echoed = apply(zs_ref).astype(BF16)
            put(rhs_ref.at[0], echoed[:, :width], echoed[:, width:])
        elif stage % 2 == 1:
            split(rows_ref[...].astype(F32) + coupling_sq * apply(zb_ref))
        else:
            split(apply(zs_ref))

    lag_l = LAG * grp
    lag_r = LAG * (n - 1 - grp)
    lag_f = jnp.maximum(lag_l, lag_r)

    def tick(t, carry):
        for lag, step in ((lag_l, left_step), (lag_r, right_step), (lag_f, full_step)):
            c = t - lag

            @pl.when(jnp.logical_and(c >= 0, c < chunks))
            def _():
                step(c)

        for stage in range(stages + 1):

            @pl.when(t == lag_f + face_chunks + LAG + stage)
            def _():
                response_stage(stage)

        return carry

    lax.fori_loop(0, chunks + LAG * (n - 1), tick, 0)

    def drain(c, carry):
        @pl.when(has_right)
        def _():
            to_right(c).wait_send()

        @pl.when(has_left)
        def _():
            to_left(c).wait_send()

        to_twin(c).wait_send()

        @pl.when(c >= face_chunks)
        def _():
            to_twin(c).wait_recv()

        return carry

    lax.fori_loop(0, chunks, drain, 0)


def product_kernel(rows, order_ref, own_ref, zb_ref, zs_ref, rhs, out_ref, held, sems):
    box = lax.axis_index("box")
    parity = lax.rem(box, 2)
    twin = box + 1 - 2 * parity
    points, width = own_ref.shape[1], own_ref.shape[2]
    face_blocks = points // BLK
    coupling_sq = 1.0 / points
    coupling = points ** (-0.5)
    ext = exterior(order_ref, box * face_blocks, width)

    per_step = rows // BLK
    steps = points // rows

    def copy_out(slot, half, order_base, block):
        row = half * points + order_ref[order_base + block] * BLK
        return pltpu.make_async_copy(
            held.at[slot], out_ref.at[:, pl.ds(pl.multiple_of(row, BLK), BLK), :], sems.at[slot]
        )

    def own_step(s, carry):
        left = zb_ref[pl.ds(pl.multiple_of(s * rows, rows), rows), :]
        prod = coupling_sq * jnp.dot(left, rhs[0], preferred_element_type=F32)
        for j in range(per_step):
            block = s * per_step + j
            row = pl.multiple_of(order_ref[box * face_blocks + block] * BLK, BLK)
            for part in range(2):
                piece = prod[j * BLK : (j + 1) * BLK, part * width : (part + 1) * width]
                held[block, part] = (
                    own_ref[part, pl.ds(row, BLK), :].astype(F32) * ext + piece
                ).astype(BF16)
            copy_out(block, parity, box * face_blocks, block).start()
        return carry

    def cross_step(s, carry):
        left = zs_ref[pl.ds(pl.multiple_of(s * rows, rows), rows), :]
        prod = -coupling * jnp.dot(left, rhs[1], preferred_element_type=F32)
        for j in range(per_step):
            block = s * per_step + j
            for part in range(2):
                piece = prod[j * BLK : (j + 1) * BLK, part * width : (part + 1) * width]
                held[face_blocks + block, part] = piece.astype(BF16)
            copy_out(face_blocks + block, 1 - parity, twin * face_blocks, block).start()
        return carry

    lax.fori_loop(0, steps, own_step, 0)
    lax.fori_loop(0, steps, cross_step, 0)

    def drain(block, carry):
        copy_out(block, parity, box * face_blocks, block).wait()
        copy_out(face_blocks + block, 1 - parity, twin * face_blocks, block).wait()
        return carry

    lax.fori_loop(0, face_blocks, drain, 0)


def shards(impedance, face_order):
    points, width = impedance.shape[3], impedance.shape[4]
    own = impedance.reshape(2, points, width)
    order = face_order.reshape(-1)
    face_blocks = points // BLK
    iface = MB * BLK
    n = lax.axis_size("grp")
    chunks = points // ROWS
    smem = pl.BlockSpec(memory_space=pltpu.SMEM)
    vmem = pl.BlockSpec(memory_space=pltpu.VMEM)
    z_shape = jax.ShapeDtypeStruct((points, 2 * iface), BF16)
    buffer = pltpu.VMEM((chunks, ROWS, 2 * iface), BF16)
    mine, rows_in = pl.pallas_call(
        pick_kernel,
        out_shape=(z_shape, jax.ShapeDtypeStruct((iface, 2 * width), BF16)),
        in_specs=[smem, vmem],
        out_specs=(vmem, vmem),
        compiler_params=pltpu.CompilerParams(vmem_limit_bytes=16 << 20),
    )(order, own)
    operand = pltpu.VMEM((2 * iface, 2 * width), BF16)
    z_own, z_twin, rhs = pl.pallas_call(
        functools.partial(gather_kernel, n),
        out_shape=(z_shape, z_shape, jax.ShapeDtypeStruct((2, 2 * iface, 2 * width), BF16)),
        in_specs=[vmem, vmem],
        out_specs=(vmem, vmem, vmem),
        scratch_shapes=[operand] * 2 + [buffer] * 4 + [pltpu.SemaphoreType.DMA((chunks,))] * 6,
        compiler_params=pltpu.CompilerParams(
            collective_id=0, has_side_effects=True, vmem_limit_bytes=40 << 20
        ),
    )(mine, rows_in)

    rows = 4 * BLK
    merged = pl.pallas_call(
        functools.partial(product_kernel, rows),
        out_shape=jax.ShapeDtypeStruct((2, 2 * points, width), BF16),
        in_specs=[smem, vmem, vmem, vmem, vmem],
        out_specs=pl.BlockSpec(memory_space=pl.ANY),
        scratch_shapes=[
            pltpu.VMEM((2 * face_blocks, 2, BLK, width), BF16),
            pltpu.SemaphoreType.DMA((2 * face_blocks,)),
        ],
        compiler_params=pltpu.CompilerParams(vmem_limit_bytes=48 << 20),
    )(order, own, z_own, z_twin, rhs)
    return merged[:, None, None]


def solution(mesh):
    in_specs = (P(None, "box", None, None, "grp"), P())
    out_specs = P(None, "box", None, None, "grp")
    return jax.shard_map(shards, mesh=mesh, in_specs=in_specs, out_specs=out_specs, check_vma=False)
```

```python
import functools

import jax
import jax.numpy as jnp
from jax import lax
from jax.experimental import pallas as pl
from jax.experimental.pallas import tpu as pltpu
from jax.sharding import PartitionSpec as P

BLK = 128
MB = 3
NS_STEPS = 2
ROWS = 64
LAG = 2
MESH_ID = pl.DeviceIdType.MESH
BF16 = jnp.bfloat16
F32 = jnp.float32


def exterior(order_ref, base, width):
    blocks = width // BLK
    first = lax.axis_index("grp") * blocks
    pieces = []
    for j in range(blocks):
        keep = order_ref[base] != first + j
        for k in range(1, MB):
            keep = jnp.logical_and(keep, order_ref[base + k] != first + j)
        pieces.append(jnp.full((1, BLK), keep.astype(F32), F32))
    return jnp.concatenate(pieces, axis=1)


def pick_kernel(order_ref, own_ref, mine_ref, rows_ref):
    width = own_ref.shape[2]
    base = lax.axis_index("box") * (own_ref.shape[1] // BLK)
    blocks = width // BLK
    first = lax.axis_index("grp") * blocks
    ext = exterior(order_ref, base, width).astype(BF16)

    def body(block, carry):
        row = pl.multiple_of(order_ref[base + block] * BLK, BLK)
        for k in range(MB):
            local = order_ref[base + k] - first
            held = jnp.logical_and(local >= 0, local < blocks).astype(F32).astype(BF16)
            col = pl.multiple_of(jnp.clip(local, 0, blocks - 1) * BLK, BLK)
            for part in range(2):
                piece = own_ref[part, pl.ds(row, BLK), pl.ds(col, BLK)]
                mine_ref[pl.ds(block * BLK, BLK), pl.ds((part * MB + k) * BLK, BLK)] = piece * held
        for part in range(2):
            rows_ref[pl.ds(block * BLK, BLK), pl.ds(part * width, width)] = (
                own_ref[part, pl.ds(row, BLK), :] * ext
            )
        return carry

    lax.fori_loop(0, own_ref.shape[1] // BLK, body, 0)


def put(dst, real, imag):
    depth, width = real.shape
    dst[pl.ds(0, depth), pl.ds(0, width)] = real
    dst[pl.ds(0, depth), pl.ds(width, width)] = imag
    dst[pl.ds(depth, depth), pl.ds(0, width)] = -imag
    dst[pl.ds(depth, depth), pl.ds(width, width)] = real


def gather_kernel(
    n, mine_ref, rows_ref, own_out, cross_out, zb_ref, zs_ref, rhs_ref, high, low, buf_l, buf_r, out_r, out_l,
    send_r, recv_l, send_l, recv_r, send_t, recv_t,
):
    box = lax.axis_index("box")
    grp = lax.axis_index("grp")
    twin = box + 1 - 2 * lax.rem(box, 2)
    chunks = buf_l.shape[0]
    has_left = grp > 0
    has_right = grp < n - 1

    barrier = pltpu.get_barrier_semaphore()
    pl.semaphore_signal(barrier, inc=1, device_id={"box": twin}, device_id_type=MESH_ID)

    @pl.when(has_left)
    def _():
        pl.semaphore_signal(barrier, inc=1, device_id={"grp": grp - 1}, device_id_type=MESH_ID)

    @pl.when(has_right)
    def _():
        pl.semaphore_signal(barrier, inc=1, device_id={"grp": grp + 1}, device_id_type=MESH_ID)

    pl.semaphore_wait(barrier, 1 + has_left.astype(jnp.int32) + has_right.astype(jnp.int32))

    def to_right(c):
        return pltpu.make_async_remote_copy(
            src_ref=out_r.at[c], dst_ref=buf_l.at[c], send_sem=send_r.at[c], recv_sem=recv_l.at[c],
            device_id={"grp": grp + 1}, device_id_type=MESH_ID,
        )

    def to_left(c):
        return pltpu.make_async_remote_copy(
            src_ref=out_l.at[c], dst_ref=buf_r.at[c], send_sem=send_l.at[c], recv_sem=recv_r.at[c],
            device_id={"grp": grp - 1}, device_id_type=MESH_ID,
        )

    def to_twin(c):
        rows = pl.ds(c * ROWS, ROWS)
        return pltpu.make_async_remote_copy(
            src_ref=zb_ref.at[rows], dst_ref=zs_ref.at[rows], send_sem=send_t.at[c], recv_sem=recv_t.at[c],
            device_id={"box": twin}, device_id_type=MESH_ID,
        )

    def mine(c):
        return mine_ref[pl.ds(pl.multiple_of(c * ROWS, ROWS), ROWS), :]

    def left_step(c):
        @pl.when(has_left)
        def _():
            to_right(c).wait_recv()

        @pl.when(jnp.logical_not(has_left))
        def _():
            buf_l[c] = jnp.zeros(buf_l.shape[1:], BF16)

        out_r[c] = mine(c) + buf_l[c]

        @pl.when(has_right)
        def _():
            to_right(c).start()

    def right_step(c):
        @pl.when(has_right)
        def _():
            to_left(c).wait_recv()

        @pl.when(jnp.logical_not(has_right))
        def _():
            buf_r[c] = jnp.zeros(buf_r.shape[1:], BF16)

        out_l[c] = mine(c) + buf_r[c]

        @pl.when(has_left)
        def _():
            to_left(c).start()

    def full_step(c):
        zb_ref[pl.ds(c * ROWS, ROWS), :] = out_r[c] + buf_r[c]
        to_twin(c).start()

    points, width = zb_ref.shape[0], rows_ref.shape[1] // 2
    coupling_sq = 1.0 / points
    coupling = points ** (-0.5)
    iface = MB * BLK

    def split(value):
        top = value.astype(BF16)
        rest = (value - top.astype(F32)).astype(BF16)
        put(high, top[:, :width], top[:, width:])
        put(low, rest[:, :width], rest[:, width:])

    def apply(z_ref):
        left = z_ref[pl.ds(0, iface), :]
        return jnp.dot(left, high[...], preferred_element_type=F32) + jnp.dot(
            left, low[...], preferred_element_type=F32
        )

    face_chunks = iface // ROWS
    stages = 2 * (2**NS_STEPS - 1)

    def response_stage(stage):
        if stage == 0:
            for c in range(face_chunks):
                to_twin(c).wait_recv()
            put(high, rows_ref[pl.ds(0, iface), pl.ds(0, width)], rows_ref[pl.ds(0, iface), pl.ds(width, width)])
            split(jnp.dot(zs_ref[pl.ds(0, iface), :], high[...], preferred_element_type=F32))
        elif stage == stages:
            rhs_ref[1] = high[...]
            echoed = apply(zs_ref).astype(BF16)
            put(rhs_ref.at[0], echoed[:, :width], echoed[:, width:])
        elif stage % 2 == 1:
            split(rows_ref[pl.ds(0, iface), :].astype(F32) + coupling_sq * apply(zb_ref))
        else:
            split(apply(zs_ref))

    per_block = BLK // ROWS
    blocks = points // BLK

    def product_step(block):
        for j in range(per_block):
            c = block * per_block + j

            @pl.when(c >= face_chunks)
            def _():
                to_twin(c).wait_recv()

        rows = pl.ds(pl.multiple_of(block * BLK, BLK), BLK)
        own = rows_ref[rows, :].astype(F32) + coupling_sq * jnp.dot(
            zb_ref[rows, :], rhs_ref[0], preferred_element_type=F32
        )
        cross = -coupling * jnp.dot(zs_ref[rows, :], rhs_ref[1], preferred_element_type=F32)
        for part in range(2):
            own_out[block, part] = own[:, part * width : (part + 1) * width].astype(BF16)
            cross_out[block, part] = cross[:, part * width : (part + 1) * width].astype(BF16)

    lag_l = LAG * grp
    lag_r = LAG * (n - 1 - grp)
    lag_f = jnp.maximum(lag_l, lag_r)

    def tick(t, done):
        for lag, step in ((lag_l, left_step), (lag_r, right_step), (lag_f, full_step)):
            c = t - lag

            @pl.when(jnp.logical_and(c >= 0, c < chunks))
            def _():
                step(c)

        for stage in range(stages + 1):

            @pl.when(t == lag_f + face_chunks + LAG + stage)
            def _():
                response_stage(stage)

        ready = jnp.logical_and(
            t > lag_f + face_chunks + LAG + stages, (done + 1) * per_block + LAG + lag_f <= t
        )
        ready = jnp.logical_and(ready, done < blocks)

        @pl.when(ready)
        def _():
            product_step(done)

        return done + ready.astype(jnp.int32)

    done = lax.fori_loop(0, chunks + LAG * (n - 1), tick, jnp.int32(0))

    def rest(block, carry):
        product_step(block)
        return carry

    lax.fori_loop(done, blocks, rest, 0)

    def drain(c, carry):
        @pl.when(has_right)
        def _():
            to_right(c).wait_send()

        @pl.when(has_left)
        def _():
            to_left(c).wait_send()

        to_twin(c).wait_send()
        return carry

    lax.fori_loop(0, chunks, drain, 0)


def place_kernel(order_ref, own_ref, cross_ref, out_ref, sems):
    box = lax.axis_index("box")
    parity = lax.rem(box, 2)
    twin = box + 1 - 2 * parity
    blocks = own_ref.shape[0]
    copies = []
    for block in range(blocks):
        for k, (src, half, order_base) in enumerate(
            ((own_ref, parity, box * blocks), (cross_ref, 1 - parity, twin * blocks))
        ):
            row = pl.multiple_of((half * blocks + order_ref[order_base + block]) * BLK, BLK)
            copy = pltpu.make_async_copy(
                src.at[block], out_ref.at[:, pl.ds(row, BLK), :], sems.at[2 * block + k]
            )
            copy.start()
            copies.append(copy)
    for copy in copies:
        copy.wait()


def shards(impedance, face_order):
    points, width = impedance.shape[3], impedance.shape[4]
    own = impedance.reshape(2, points, width)
    order = face_order.reshape(-1)
    face_blocks = points // BLK
    iface = MB * BLK
    n = lax.axis_size("grp")
    chunks = points // ROWS
    smem = pl.BlockSpec(memory_space=pltpu.SMEM)
    vmem = pl.BlockSpec(memory_space=pltpu.VMEM)
    z_shape = jax.ShapeDtypeStruct((points, 2 * iface), BF16)
    buffer = pltpu.VMEM((chunks, ROWS, 2 * iface), BF16)
    mine, rows_in = pl.pallas_call(
        pick_kernel,
        out_shape=(z_shape, jax.ShapeDtypeStruct((points, 2 * width), BF16)),
        in_specs=[smem, vmem],
        out_specs=(vmem, vmem),
        compiler_params=pltpu.CompilerParams(vmem_limit_bytes=16 << 20),
    )(order, own)
    operand = pltpu.VMEM((2 * iface, 2 * width), BF16)
    out_shape = jax.ShapeDtypeStruct((face_blocks, 2, BLK, width), BF16)
    own_out, cross_out = pl.pallas_call(
        functools.partial(gather_kernel, n),
        out_shape=(out_shape, out_shape),
        in_specs=[vmem, vmem],
        out_specs=(vmem, vmem),
        scratch_shapes=[pltpu.VMEM((points, 2 * iface), BF16)] * 2
        + [pltpu.VMEM((2, 2 * iface, 2 * width), BF16)]
        + [operand] * 2
        + [buffer] * 4 + [pltpu.SemaphoreType.DMA((chunks,))] * 6,
        compiler_params=pltpu.CompilerParams(
            collective_id=0, has_side_effects=True, vmem_limit_bytes=36 << 20
        ),
    )(mine, rows_in)

    merged = pl.pallas_call(
        place_kernel,
        out_shape=jax.ShapeDtypeStruct((2, 2 * points, width), BF16),
        in_specs=[smem, vmem, vmem],
        out_specs=pl.BlockSpec(memory_space=pl.ANY),
        scratch_shapes=[pltpu.SemaphoreType.DMA((2 * face_blocks,))],
        compiler_params=pltpu.CompilerParams(vmem_limit_bytes=16 << 20),
    )(order, own_out, cross_out)
    return merged[:, None, None]


def solution(mesh):
    in_specs = (P(None, "box", None, None, "grp"), P())
    out_specs = P(None, "box", None, None, "grp")
    return jax.shard_map(shards, mesh=mesh, in_specs=in_specs, out_specs=out_specs, check_vma=False)
```

```python
import functools

import jax
import jax.numpy as jnp
from jax import lax
from jax.experimental import pallas as pl
from jax.experimental.pallas import tpu as pltpu
from jax.sharding import PartitionSpec as P

BLK = 128
MB = 3
NS_STEPS = 2
ROWS = 32
LAG = 2
STRIDE = 2
MESH_ID = pl.DeviceIdType.MESH
BF16 = jnp.bfloat16
F32 = jnp.float32


def exterior(order_ref, base, width):
    blocks = width // BLK
    first = lax.axis_index("grp") * blocks
    pieces = []
    for j in range(blocks):
        keep = order_ref[base, 0, 0] != first + j
        for k in range(1, MB):
            keep = jnp.logical_and(keep, order_ref[base, 0, k] != first + j)
        pieces.append(jnp.full((1, BLK), keep.astype(F32), F32))
    return jnp.concatenate(pieces, axis=1)


def pick_kernel(order_ref, own_ref, mine_ref, rows_ref):
    width = own_ref.shape[2]
    base = lax.axis_index("box")
    blocks = width // BLK
    first = lax.axis_index("grp") * blocks
    ext = exterior(order_ref, base, width).astype(BF16)

    def body(block, carry):
        row = pl.multiple_of(order_ref[base, 0, block] * BLK, BLK)
        for k in range(MB):
            local = order_ref[base, 0, k] - first
            held = jnp.logical_and(local >= 0, local < blocks).astype(F32).astype(BF16)
            col = pl.multiple_of(jnp.clip(local, 0, blocks - 1) * BLK, BLK)
            for part in range(2):
                piece = own_ref[part, pl.ds(row, BLK), pl.ds(col, BLK)]
                mine_ref[pl.ds(block * BLK, BLK), pl.ds((part * MB + k) * BLK, BLK)] = piece * held
        for part in range(2):
            rows_ref[pl.ds(block * BLK, BLK), pl.ds(part * width, width)] = (
                own_ref[part, pl.ds(row, BLK), :] * ext
            )
        return carry

    lax.fori_loop(0, own_ref.shape[1] // BLK, body, 0)


def put(dst, real, imag):
    depth, width = real.shape
    dst[pl.ds(0, depth), pl.ds(0, width)] = real
    dst[pl.ds(0, depth), pl.ds(width, width)] = imag
    dst[pl.ds(depth, depth), pl.ds(0, width)] = -imag
    dst[pl.ds(depth, depth), pl.ds(width, width)] = real


def gather_kernel(
    n, mine_ref, rows_ref, own_out, cross_out, zb_ref, zs_ref, rhs_ref, high, low, buf_l, buf_r, out_r, out_l,
    send_r, recv_l, send_l, recv_r, send_t, recv_t,
):
    box = lax.axis_index("box")
    grp = lax.axis_index("grp")
    twin = box + 1 - 2 * lax.rem(box, 2)
    chunks = buf_l.shape[0]
    has_left = grp > 0
    has_right = grp < n - 1

    barrier = pltpu.get_barrier_semaphore()
    pl.semaphore_signal(barrier, inc=1, device_id={"box": twin}, device_id_type=MESH_ID)

    @pl.when(has_left)
    def _():
        pl.semaphore_signal(barrier, inc=1, device_id={"grp": grp - 1}, device_id_type=MESH_ID)

    @pl.when(has_right)
    def _():
        pl.semaphore_signal(barrier, inc=1, device_id={"grp": grp + 1}, device_id_type=MESH_ID)

    pl.semaphore_wait(barrier, 1 + has_left.astype(jnp.int32) + has_right.astype(jnp.int32))

    def to_right(c):
        return pltpu.make_async_remote_copy(
            src_ref=out_r.at[c], dst_ref=buf_l.at[c], send_sem=send_r.at[c], recv_sem=recv_l.at[c],
            device_id={"grp": grp + 1}, device_id_type=MESH_ID,
        )

    def to_left(c):
        return pltpu.make_async_remote_copy(
            src_ref=out_l.at[c], dst_ref=buf_r.at[c], send_sem=send_l.at[c], recv_sem=recv_r.at[c],
            device_id={"grp": grp - 1}, device_id_type=MESH_ID,
        )

    def to_twin(c):
        rows = pl.ds(c * ROWS, ROWS)
        return pltpu.make_async_remote_copy(
            src_ref=zb_ref.at[rows], dst_ref=zs_ref.at[rows], send_sem=send_t.at[c], recv_sem=recv_t.at[c],
            device_id={"box": twin}, device_id_type=MESH_ID,
        )

    def mine(c):
        return mine_ref[pl.ds(pl.multiple_of(c * ROWS, ROWS), ROWS), :]

    def left_step(c):
        @pl.when(has_left)
        def _():
            to_right(c).wait_recv()

        @pl.when(jnp.logical_not(has_left))
        def _():
            buf_l[c] = jnp.zeros(buf_l.shape[1:], BF16)

        out_r[c] = mine(c) + buf_l[c]

        @pl.when(has_right)
        def _():
            to_right(c).start()

    def right_step(c):
        @pl.when(has_right)
        def _():
            to_left(c).wait_recv()

        @pl.when(jnp.logical_not(has_right))
        def _():
            buf_r[c] = jnp.zeros(buf_r.shape[1:], BF16)

        out_l[c] = mine(c) + buf_r[c]

        @pl.when(has_left)
        def _():
            to_left(c).start()

    def full_step(c):
        zb_ref[pl.ds(c * ROWS, ROWS), :] = out_r[c] + buf_r[c]
        to_twin(c).start()

    points, width = zb_ref.shape[0], rows_ref.shape[1] // 2
    coupling_sq = 1.0 / points
    coupling = points ** (-0.5)
    iface = MB * BLK

    def split(value):
        top = value.astype(BF16)
        rest = (value - top.astype(F32)).astype(BF16)
        put(high, top[:, :width], top[:, width:])
        put(low, rest[:, :width], rest[:, width:])

    def apply(z_ref):
        left = z_ref[pl.ds(0, iface), :]
        return jnp.dot(left, high[...], preferred_element_type=F32) + jnp.dot(
            left, low[...], preferred_element_type=F32
        )

    face_chunks = iface // ROWS
    stages = 2 * (2**NS_STEPS - 1)

    def response_stage(stage):
        if stage == 0:
            for c in range(face_chunks):
                to_twin(c).wait_recv()
            put(high, rows_ref[pl.ds(0, iface), pl.ds(0, width)], rows_ref[pl.ds(0, iface), pl.ds(width, width)])
            split(jnp.dot(zs_ref[pl.ds(0, iface), :], high[...], preferred_element_type=F32))
        elif stage == stages:
            rhs_ref[1] = high[...]
            echoed = apply(zs_ref).astype(BF16)
            put(rhs_ref.at[0], echoed[:, :width], echoed[:, width:])
        elif stage % 2 == 1:
            split(rows_ref[pl.ds(0, iface), :].astype(F32) + coupling_sq * apply(zb_ref))
        else:
            split(apply(zs_ref))

    per_block = BLK // ROWS
    blocks = points // BLK

    def product_step(block):
        for j in range(per_block):
            c = block * per_block + j

            @pl.when(c >= face_chunks)
            def _():
                to_twin(c).wait_recv()

        rows = pl.ds(pl.multiple_of(block * BLK, BLK), BLK)
        own = rows_ref[rows, :].astype(F32) + coupling_sq * jnp.dot(
            zb_ref[rows, :], rhs_ref[0], preferred_element_type=F32
        )
        cross = -coupling * jnp.dot(zs_ref[rows, :], rhs_ref[1], preferred_element_type=F32)
        for part in range(2):
            own_out[block, part] = own[:, part * width : (part + 1) * width].astype(BF16)
            cross_out[block, part] = cross[:, part * width : (part + 1) * width].astype(BF16)

    lag_l = LAG * grp
    lag_r = LAG * (n - 1 - grp)
    lag_f = jnp.maximum(lag_l, lag_r)

    def tick(t, done):
        for lag, step in ((lag_l, left_step), (lag_r, right_step), (lag_f, full_step)):
            c = t - lag

            @pl.when(jnp.logical_and(c >= 0, c < chunks))
            def _():
                step(c)

        for stage in range(stages + 1):

            @pl.when(t == lag_f + face_chunks + LAG + STRIDE * stage)
            def _():
                response_stage(stage)

        ready = jnp.logical_and(
            t > lag_f + face_chunks + LAG + STRIDE * stages, (done + 1) * per_block + LAG + lag_f <= t
        )
        ready = jnp.logical_and(ready, jnp.logical_and(done < blocks, lax.rem(t, STRIDE) == 0))

        @pl.when(ready)
        def _():
            product_step(done)

        return done + ready.astype(jnp.int32)

    done = lax.fori_loop(0, chunks + LAG * (n - 1), tick, jnp.int32(0))

    def rest(block, carry):
        product_step(block)
        return carry

    lax.fori_loop(done, blocks, rest, 0)

    def drain(c, carry):
        @pl.when(has_right)
        def _():
            to_right(c).wait_send()

        @pl.when(has_left)
        def _():
            to_left(c).wait_send()

        to_twin(c).wait_send()
        return carry

    lax.fori_loop(0, chunks, drain, 0)


def place_kernel(order_ref, own_ref, cross_ref, out_ref, sems):
    box = lax.axis_index("box")
    parity = lax.rem(box, 2)
    twin = box + 1 - 2 * parity
    blocks = own_ref.shape[0]
    copies = []
    for block in range(blocks):
        for k, (src, half, order_base) in enumerate(
            ((own_ref, parity, box), (cross_ref, 1 - parity, twin))
        ):
            row = pl.multiple_of((half * blocks + order_ref[order_base, 0, block]) * BLK, BLK)
            copy = pltpu.make_async_copy(
                src.at[block], out_ref.at[:, pl.ds(row, BLK), :], sems.at[2 * block + k]
            )
            copy.start()
            copies.append(copy)
    for copy in copies:
        copy.wait()


def shards(impedance, face_order):
    points, width = impedance.shape[3], impedance.shape[4]
    own = impedance.reshape(2, points, width)
    face_blocks = points // BLK
    iface = MB * BLK
    n = lax.axis_size("grp")
    chunks = points // ROWS
    smem = pl.BlockSpec(memory_space=pltpu.SMEM)
    vmem = pl.BlockSpec(memory_space=pltpu.VMEM)
    z_shape = jax.ShapeDtypeStruct((points, 2 * iface), BF16)
    buffer = pltpu.VMEM((chunks, ROWS, 2 * iface), BF16)
    mine, rows_in = pl.pallas_call(
        pick_kernel,
        out_shape=(z_shape, jax.ShapeDtypeStruct((points, 2 * width), BF16)),
        in_specs=[smem, vmem],
        out_specs=(vmem, vmem),
        compiler_params=pltpu.CompilerParams(vmem_limit_bytes=16 << 20),
    )(face_order, own)
    operand = pltpu.VMEM((2 * iface, 2 * width), BF16)
    out_shape = jax.ShapeDtypeStruct((face_blocks, 2, BLK, width), BF16)
    own_out, cross_out = pl.pallas_call(
        functools.partial(gather_kernel, n),
        out_shape=(out_shape, out_shape),
        in_specs=[vmem, vmem],
        out_specs=(vmem, vmem),
        scratch_shapes=[pltpu.VMEM((points, 2 * iface), BF16)] * 2
        + [pltpu.VMEM((2, 2 * iface, 2 * width), BF16)]
        + [operand] * 2
        + [buffer] * 4 + [pltpu.SemaphoreType.DMA((chunks,))] * 6,
        compiler_params=pltpu.CompilerParams(
            collective_id=0, has_side_effects=True, vmem_limit_bytes=36 << 20
        ),
    )(mine, rows_in)

    merged = pl.pallas_call(
        place_kernel,
        out_shape=jax.ShapeDtypeStruct((2, 2 * points, width), BF16),
        in_specs=[smem, vmem, vmem],
        out_specs=pl.BlockSpec(memory_space=pl.ANY),
        scratch_shapes=[pltpu.SemaphoreType.DMA((2 * face_blocks,))],
        compiler_params=pltpu.CompilerParams(vmem_limit_bytes=16 << 20),
    )(face_order, own_out, cross_out)
    return merged[:, None, None]


def solution(mesh):
    in_specs = (P(None, "box", None, None, "grp"), P())
    out_specs = P(None, "box", None, None, "grp")
    return jax.shard_map(shards, mesh=mesh, in_specs=in_specs, out_specs=out_specs, check_vma=False)
```

```python
import functools

import jax
import jax.numpy as jnp
from jax import lax
from jax.experimental import pallas as pl
from jax.experimental.pallas import tpu as pltpu
from jax.sharding import PartitionSpec as P

BLK = 128
MB = 3
NS_STEPS = 2
ROWS = 64
LAG = 2
STRIDE = 1
MESH_ID = pl.DeviceIdType.MESH
BF16 = jnp.bfloat16
F32 = jnp.float32


def exterior(order_ref, base, width):
    blocks = width // BLK
    first = lax.axis_index("grp") * blocks
    pieces = []
    for j in range(blocks):
        keep = order_ref[base, 0, 0] != first + j
        for k in range(1, MB):
            keep = jnp.logical_and(keep, order_ref[base, 0, k] != first + j)
        pieces.append(jnp.full((1, BLK), keep.astype(F32), F32))
    return jnp.concatenate(pieces, axis=1)


def pick_kernel(order_ref, own_ref, mine_ref, rows_ref):
    width = own_ref.shape[2]
    base = lax.axis_index("box")
    blocks = width // BLK
    first = lax.axis_index("grp") * blocks
    ext = exterior(order_ref, base, width).astype(BF16)

    def body(block, carry):
        row = pl.multiple_of(order_ref[base, 0, block] * BLK, BLK)
        for k in range(MB):
            local = order_ref[base, 0, k] - first
            held = jnp.logical_and(local >= 0, local < blocks).astype(F32).astype(BF16)
            col = pl.multiple_of(jnp.clip(local, 0, blocks - 1) * BLK, BLK)
            for part in range(2):
                piece = own_ref[part, pl.ds(row, BLK), pl.ds(col, BLK)]
                mine_ref[pl.ds(block * BLK, BLK), pl.ds((part * MB + k) * BLK, BLK)] = piece * held
        for part in range(2):
            rows_ref[pl.ds(block * BLK, BLK), pl.ds(part * width, width)] = (
                own_ref[part, pl.ds(row, BLK), :] * ext
            )
        return carry

    lax.fori_loop(0, own_ref.shape[1] // BLK, body, 0)


def put(dst, real, imag):
    depth, width = real.shape
    dst[pl.ds(0, depth), pl.ds(0, width)] = real
    dst[pl.ds(0, depth), pl.ds(width, width)] = imag
    dst[pl.ds(depth, depth), pl.ds(0, width)] = -imag
    dst[pl.ds(depth, depth), pl.ds(width, width)] = real


def gather_kernel(
    n, mine_ref, rows_ref, own_out, cross_out, zb_ref, zs_ref, rhs_ref, high, low, buf_l, buf_r, out_r, out_l,
    send_r, recv_l, send_l, recv_r, send_t, recv_t,
):
    box = lax.axis_index("box")
    grp = lax.axis_index("grp")
    twin = box + 1 - 2 * lax.rem(box, 2)
    chunks = buf_l.shape[0]
    has_left = grp > 0
    has_right = grp < n - 1

    barrier = pltpu.get_barrier_semaphore()
    pl.semaphore_signal(barrier, inc=1, device_id={"box": twin}, device_id_type=MESH_ID)

    @pl.when(has_left)
    def _():
        pl.semaphore_signal(barrier, inc=1, device_id={"grp": grp - 1}, device_id_type=MESH_ID)

    @pl.when(has_right)
    def _():
        pl.semaphore_signal(barrier, inc=1, device_id={"grp": grp + 1}, device_id_type=MESH_ID)

    pl.semaphore_wait(barrier, 1 + has_left.astype(jnp.int32) + has_right.astype(jnp.int32))

    def to_right(c):
        return pltpu.make_async_remote_copy(
            src_ref=out_r.at[c], dst_ref=buf_l.at[c], send_sem=send_r.at[c], recv_sem=recv_l.at[c],
            device_id={"grp": grp + 1}, device_id_type=MESH_ID,
        )

    def to_left(c):
        return pltpu.make_async_remote_copy(
            src_ref=out_l.at[c], dst_ref=buf_r.at[c], send_sem=send_l.at[c], recv_sem=recv_r.at[c],
            device_id={"grp": grp - 1}, device_id_type=MESH_ID,
        )

    def to_twin(c):
        rows = pl.ds(c * ROWS, ROWS)
        return pltpu.make_async_remote_copy(
            src_ref=zb_ref.at[rows], dst_ref=zs_ref.at[rows], send_sem=send_t.at[c], recv_sem=recv_t.at[c],
            device_id={"box": twin}, device_id_type=MESH_ID,
        )

    def mine(c):
        return mine_ref[pl.ds(pl.multiple_of(c * ROWS, ROWS), ROWS), :]

    def left_step(c):
        @pl.when(has_left)
        def _():
            to_right(c).wait_recv()

        @pl.when(jnp.logical_not(has_left))
        def _():
            buf_l[c] = jnp.zeros(buf_l.shape[1:], BF16)

        out_r[c] = mine(c) + buf_l[c]

        @pl.when(has_right)
        def _():
            to_right(c).start()

    def right_step(c):
        @pl.when(has_right)
        def _():
            to_left(c).wait_recv()

        @pl.when(jnp.logical_not(has_right))
        def _():
            buf_r[c] = jnp.zeros(buf_r.shape[1:], BF16)

        out_l[c] = mine(c) + buf_r[c]

        @pl.when(has_left)
        def _():
            to_left(c).start()

    def full_step(c):
        zb_ref[pl.ds(c * ROWS, ROWS), :] = out_r[c] + buf_r[c]
        to_twin(c).start()

    points, width = zb_ref.shape[0], rows_ref.shape[1] // 2
    coupling_sq = 1.0 / points
    coupling = points ** (-0.5)
    iface = MB * BLK

    def split(value):
        top = value.astype(BF16)
        rest = (value - top.astype(F32)).astype(BF16)
        put(high, top[:, :width], top[:, width:])
        put(low, rest[:, :width], rest[:, width:])

    def apply(z_ref):
        left = z_ref[pl.ds(0, iface), :]
        return jnp.dot(left, high[...], preferred_element_type=F32) + jnp.dot(
            left, low[...], preferred_element_type=F32
        )

    face_chunks = iface // ROWS
    stages = 2 * (2**NS_STEPS - 1)

    def response_stage(stage):
        if stage == 0:
            for c in range(face_chunks):
                to_twin(c).wait_recv()
            put(high, rows_ref[pl.ds(0, iface), pl.ds(0, width)], rows_ref[pl.ds(0, iface), pl.ds(width, width)])
            split(jnp.dot(zs_ref[pl.ds(0, iface), :], high[...], preferred_element_type=F32))
        elif stage == stages:
            rhs_ref[1] = high[...]
            echoed = apply(zs_ref).astype(BF16)
            put(rhs_ref.at[0], echoed[:, :width], echoed[:, width:])
        elif stage % 2 == 1:
            split(rows_ref[pl.ds(0, iface), :].astype(F32) + coupling_sq * apply(zb_ref))
        else:
            split(apply(zs_ref))

    per_block = BLK // ROWS
    blocks = points // BLK

    def product_step(block):
        for j in range(per_block):
            c = block * per_block + j

            @pl.when(c >= face_chunks)
            def _():
                to_twin(c).wait_recv()

        rows = pl.ds(pl.multiple_of(block * BLK, BLK), BLK)
        own = rows_ref[rows, :].astype(F32) + coupling_sq * jnp.dot(
            zb_ref[rows, :], rhs_ref[0], preferred_element_type=F32
        )
        cross = -coupling * jnp.dot(zs_ref[rows, :], rhs_ref[1], preferred_element_type=F32)
        for part in range(2):
            own_out[block, part] = own[:, part * width : (part + 1) * width].astype(BF16)
            cross_out[block, part] = cross[:, part * width : (part + 1) * width].astype(BF16)

    lag_l = LAG * grp
    lag_r = LAG * (n - 1 - grp)
    lag_f = jnp.maximum(lag_l, lag_r)

    def tick(t, done):
        for lag, step in ((lag_l, left_step), (lag_r, right_step), (lag_f, full_step)):
            c = t - lag

            @pl.when(jnp.logical_and(c >= 0, c < chunks))
            def _():
                step(c)

        for stage in range(stages + 1):

            @pl.when(t == lag_f + face_chunks + LAG + STRIDE * stage)
            def _():
                response_stage(stage)

        ready = jnp.logical_and(
            t > lag_f + face_chunks + LAG + STRIDE * stages, (done + 1) * per_block + LAG + lag_f <= t
        )
        ready = jnp.logical_and(ready, jnp.logical_and(done < blocks, lax.rem(t, STRIDE) == 0))

        @pl.when(ready)
        def _():
            product_step(done)

        return done + ready.astype(jnp.int32)

    done = lax.fori_loop(0, chunks + LAG * (n - 1), tick, jnp.int32(0))

    def rest(block, carry):
        product_step(block)
        return carry

    lax.fori_loop(done, blocks, rest, 0)

    def drain(c, carry):
        @pl.when(has_right)
        def _():
            to_right(c).wait_send()

        @pl.when(has_left)
        def _():
            to_left(c).wait_send()

        to_twin(c).wait_send()
        return carry

    lax.fori_loop(0, chunks, drain, 0)


def place_kernel(order_ref, own_ref, cross_ref, out_ref, sems):
    box = lax.axis_index("box")
    parity = lax.rem(box, 2)
    twin = box + 1 - 2 * parity
    blocks = own_ref.shape[0]
    copies = []
    for block in range(blocks):
        for k, (src, half, order_base) in enumerate(
            ((own_ref, parity, box), (cross_ref, 1 - parity, twin))
        ):
            row = pl.multiple_of((half * blocks + order_ref[order_base, 0, block]) * BLK, BLK)
            copy = pltpu.make_async_copy(
                src.at[block], out_ref.at[:, pl.ds(row, BLK), :], sems.at[2 * block + k]
            )
            copy.start()
            copies.append(copy)
    for copy in copies:
        copy.wait()


def shards(impedance, face_order):
    points, width = impedance.shape[3], impedance.shape[4]
    own = impedance.reshape(2, points, width)
    face_blocks = points // BLK
    iface = MB * BLK
    n = lax.axis_size("grp")
    chunks = points // ROWS
    smem = pl.BlockSpec(memory_space=pltpu.SMEM)
    vmem = pl.BlockSpec(memory_space=pltpu.VMEM)
    z_shape = jax.ShapeDtypeStruct((points, 2 * iface), BF16)
    buffer = pltpu.VMEM((chunks, ROWS, 2 * iface), BF16)
    mine, rows_in = pl.pallas_call(
        pick_kernel,
        out_shape=(z_shape, jax.ShapeDtypeStruct((points, 2 * width), BF16)),
        in_specs=[smem, vmem],
        out_specs=(vmem, vmem),
        compiler_params=pltpu.CompilerParams(vmem_limit_bytes=16 << 20),
    )(face_order, own)
    operand = pltpu.VMEM((2 * iface, 2 * width), BF16)
    out_shape = jax.ShapeDtypeStruct((face_blocks, 2, BLK, width), BF16)
    own_out, cross_out = pl.pallas_call(
        functools.partial(gather_kernel, n),
        out_shape=(out_shape, out_shape),
        in_specs=[vmem, vmem],
        out_specs=(vmem, vmem),
        scratch_shapes=[pltpu.VMEM((points, 2 * iface), BF16)] * 2
        + [pltpu.VMEM((2, 2 * iface, 2 * width), BF16)]
        + [operand] * 2
        + [buffer] * 4 + [pltpu.SemaphoreType.DMA((chunks,))] * 6,
        compiler_params=pltpu.CompilerParams(
            collective_id=0, has_side_effects=True, vmem_limit_bytes=36 << 20
        ),
    )(mine, rows_in)

    merged = pl.pallas_call(
        place_kernel,
        out_shape=jax.ShapeDtypeStruct((2, 2 * points, width), BF16),
        in_specs=[smem, vmem, vmem],
        out_specs=pl.BlockSpec(memory_space=pl.ANY),
        scratch_shapes=[pltpu.SemaphoreType.DMA((2 * face_blocks,))],
        compiler_params=pltpu.CompilerParams(vmem_limit_bytes=16 << 20),
    )(face_order, own_out, cross_out)
    return merged[:, None, None]


def solution(mesh):
    in_specs = (P(None, "box", None, None, "grp"), P())
    out_specs = P(None, "box", None, None, "grp")
    return jax.shard_map(shards, mesh=mesh, in_specs=in_specs, out_specs=out_specs, check_vma=False)
```

```python
import functools

import jax
import jax.numpy as jnp
from jax import lax
from jax.experimental import pallas as pl
from jax.experimental.pallas import tpu as pltpu
from jax.sharding import PartitionSpec as P

BLK = 128
MB = 3
NS_STEPS = 2
ROWS = 32
LAG = 3
STRIDE = 2
MESH_ID = pl.DeviceIdType.MESH
BF16 = jnp.bfloat16
F32 = jnp.float32


def exterior(order_ref, base, width):
    blocks = width // BLK
    first = lax.axis_index("grp") * blocks
    pieces = []
    for j in range(blocks):
        keep = order_ref[base, 0, 0] != first + j
        for k in range(1, MB):
            keep = jnp.logical_and(keep, order_ref[base, 0, k] != first + j)
        pieces.append(jnp.full((1, BLK), keep.astype(F32), F32))
    return jnp.concatenate(pieces, axis=1)


def pick_kernel(order_ref, own_ref, mine_ref, rows_ref):
    width = own_ref.shape[2]
    base = lax.axis_index("box")
    blocks = width // BLK
    first = lax.axis_index("grp") * blocks
    ext = exterior(order_ref, base, width).astype(BF16)

    def body(block, carry):
        row = pl.multiple_of(order_ref[base, 0, block] * BLK, BLK)
        for k in range(MB):
            local = order_ref[base, 0, k] - first
            held = jnp.logical_and(local >= 0, local < blocks).astype(F32).astype(BF16)
            col = pl.multiple_of(jnp.clip(local, 0, blocks - 1) * BLK, BLK)
            for part in range(2):
                piece = own_ref[part, pl.ds(row, BLK), pl.ds(col, BLK)]
                mine_ref[pl.ds(block * BLK, BLK), pl.ds((part * MB + k) * BLK, BLK)] = piece * held
        for part in range(2):
            rows_ref[pl.ds(block * BLK, BLK), pl.ds(part * width, width)] = (
                own_ref[part, pl.ds(row, BLK), :] * ext
            )
        return carry

    lax.fori_loop(0, own_ref.shape[1] // BLK, body, 0)


def put(dst, real, imag):
    depth, width = real.shape
    dst[pl.ds(0, depth), pl.ds(0, width)] = real
    dst[pl.ds(0, depth), pl.ds(width, width)] = imag
    dst[pl.ds(depth, depth), pl.ds(0, width)] = -imag
    dst[pl.ds(depth, depth), pl.ds(width, width)] = real


def gather_kernel(
    n, mine_ref, rows_ref, own_out, cross_out, zb_ref, zs_ref, rhs_ref, high, low, buf_l, buf_r, out_r, out_l,
    send_r, recv_l, send_l, recv_r, send_t, recv_t,
):
    box = lax.axis_index("box")
    grp = lax.axis_index("grp")
    twin = box + 1 - 2 * lax.rem(box, 2)
    chunks = buf_l.shape[0]
    has_left = grp > 0
    has_right = grp < n - 1

    barrier = pltpu.get_barrier_semaphore()
    pl.semaphore_signal(barrier, inc=1, device_id={"box": twin}, device_id_type=MESH_ID)

    @pl.when(has_left)
    def _():
        pl.semaphore_signal(barrier, inc=1, device_id={"grp": grp - 1}, device_id_type=MESH_ID)

    @pl.when(has_right)
    def _():
        pl.semaphore_signal(barrier, inc=1, device_id={"grp": grp + 1}, device_id_type=MESH_ID)

    pl.semaphore_wait(barrier, 1 + has_left.astype(jnp.int32) + has_right.astype(jnp.int32))

    def to_right(c):
        return pltpu.make_async_remote_copy(
            src_ref=out_r.at[c], dst_ref=buf_l.at[c], send_sem=send_r.at[c], recv_sem=recv_l.at[c],
            device_id={"grp": grp + 1}, device_id_type=MESH_ID,
        )

    def to_left(c):
        return pltpu.make_async_remote_copy(
            src_ref=out_l.at[c], dst_ref=buf_r.at[c], send_sem=send_l.at[c], recv_sem=recv_r.at[c],
            device_id={"grp": grp - 1}, device_id_type=MESH_ID,
        )

    def to_twin(c):
        rows = pl.ds(c * ROWS, ROWS)
        return pltpu.make_async_remote_copy(
            src_ref=zb_ref.at[rows], dst_ref=zs_ref.at[rows], send_sem=send_t.at[c], recv_sem=recv_t.at[c],
            device_id={"box": twin}, device_id_type=MESH_ID,
        )

    def mine(c):
        return mine_ref[pl.ds(pl.multiple_of(c * ROWS, ROWS), ROWS), :]

    def left_step(c):
        @pl.when(has_left)
        def _():
            to_right(c).wait_recv()

        @pl.when(jnp.logical_not(has_left))
        def _():
            buf_l[c] = jnp.zeros(buf_l.shape[1:], BF16)

        out_r[c] = mine(c) + buf_l[c]

        @pl.when(has_right)
        def _():
            to_right(c).start()

    def right_step(c):
        @pl.when(has_right)
        def _():
            to_left(c).wait_recv()

        @pl.when(jnp.logical_not(has_right))
        def _():
            buf_r[c] = jnp.zeros(buf_r.shape[1:], BF16)

        out_l[c] = mine(c) + buf_r[c]

        @pl.when(has_left)
        def _():
            to_left(c).start()

    def full_step(c):
        zb_ref[pl.ds(c * ROWS, ROWS), :] = out_r[c] + buf_r[c]
        to_twin(c).start()

    points, width = zb_ref.shape[0], rows_ref.shape[1] // 2
    coupling_sq = 1.0 / points
    coupling = points ** (-0.5)
    iface = MB * BLK

    def split(value):
        top = value.astype(BF16)
        rest = (value - top.astype(F32)).astype(BF16)
        put(high, top[:, :width], top[:, width:])
        put(low, rest[:, :width], rest[:, width:])

    def apply(z_ref):
        left = z_ref[pl.ds(0, iface), :]
        return jnp.dot(left, high[...], preferred_element_type=F32) + jnp.dot(
            left, low[...], preferred_element_type=F32
        )

    face_chunks = iface // ROWS
    stages = 2 * (2**NS_STEPS - 1)

    def response_stage(stage):
        if stage == 0:
            for c in range(face_chunks):
                to_twin(c).wait_recv()
            put(high, rows_ref[pl.ds(0, iface), pl.ds(0, width)], rows_ref[pl.ds(0, iface), pl.ds(width, width)])
            split(jnp.dot(zs_ref[pl.ds(0, iface), :], high[...], preferred_element_type=F32))
        elif stage == stages:
            rhs_ref[1] = high[...]
            echoed = apply(zs_ref).astype(BF16)
            put(rhs_ref.at[0], echoed[:, :width], echoed[:, width:])
        elif stage % 2 == 1:
            split(rows_ref[pl.ds(0, iface), :].astype(F32) + coupling_sq * apply(zb_ref))
        else:
            split(apply(zs_ref))

    per_block = BLK // ROWS
    blocks = points // BLK

    def product_step(block):
        for j in range(per_block):
            c = block * per_block + j

            @pl.when(c >= face_chunks)
            def _():
                to_twin(c).wait_recv()

        rows = pl.ds(pl.multiple_of(block * BLK, BLK), BLK)
        own = rows_ref[rows, :].astype(F32) + coupling_sq * jnp.dot(
            zb_ref[rows, :], rhs_ref[0], preferred_element_type=F32
        )
        cross = -coupling * jnp.dot(zs_ref[rows, :], rhs_ref[1], preferred_element_type=F32)
        for part in range(2):
            own_out[block, part] = own[:, part * width : (part + 1) * width].astype(BF16)
            cross_out[block, part] = cross[:, part * width : (part + 1) * width].astype(BF16)

    lag_l = LAG * grp
    lag_r = LAG * (n - 1 - grp)
    lag_f = jnp.maximum(lag_l, lag_r)

    def tick(t, done):
        for lag, step in ((lag_l, left_step), (lag_r, right_step), (lag_f, full_step)):
            c = t - lag

            @pl.when(jnp.logical_and(c >= 0, c < chunks))
            def _():
                step(c)

        for stage in range(stages + 1):

            @pl.when(t == lag_f + face_chunks + LAG + STRIDE * stage)
            def _():
                response_stage(stage)

        ready = jnp.logical_and(
            t > lag_f + face_chunks + LAG + STRIDE * stages, (done + 1) * per_block + LAG + lag_f <= t
        )
        ready = jnp.logical_and(ready, jnp.logical_and(done < blocks, lax.rem(t, STRIDE) == 0))

        @pl.when(ready)
        def _():
            product_step(done)

        return done + ready.astype(jnp.int32)

    done = lax.fori_loop(0, chunks + LAG * (n - 1), tick, jnp.int32(0))

    def rest(block, carry):
        product_step(block)
        return carry

    lax.fori_loop(done, blocks, rest, 0)

    def drain(c, carry):
        @pl.when(has_right)
        def _():
            to_right(c).wait_send()

        @pl.when(has_left)
        def _():
            to_left(c).wait_send()

        to_twin(c).wait_send()
        return carry

    lax.fori_loop(0, chunks, drain, 0)


def place_kernel(order_ref, own_ref, cross_ref, out_ref, sems):
    box = lax.axis_index("box")
    parity = lax.rem(box, 2)
    twin = box + 1 - 2 * parity
    blocks = own_ref.shape[0]
    copies = []
    for block in range(blocks):
        for k, (src, half, order_base) in enumerate(
            ((own_ref, parity, box), (cross_ref, 1 - parity, twin))
        ):
            row = pl.multiple_of((half * blocks + order_ref[order_base, 0, block]) * BLK, BLK)
            copy = pltpu.make_async_copy(
                src.at[block], out_ref.at[:, pl.ds(row, BLK), :], sems.at[2 * block + k]
            )
            copy.start()
            copies.append(copy)
    for copy in copies:
        copy.wait()


def shards(impedance, face_order):
    points, width = impedance.shape[3], impedance.shape[4]
    own = impedance.reshape(2, points, width)
    face_blocks = points // BLK
    iface = MB * BLK
    n = lax.axis_size("grp")
    chunks = points // ROWS
    smem = pl.BlockSpec(memory_space=pltpu.SMEM)
    vmem = pl.BlockSpec(memory_space=pltpu.VMEM)
    z_shape = jax.ShapeDtypeStruct((points, 2 * iface), BF16)
    buffer = pltpu.VMEM((chunks, ROWS, 2 * iface), BF16)
    mine, rows_in = pl.pallas_call(
        pick_kernel,
        out_shape=(z_shape, jax.ShapeDtypeStruct((points, 2 * width), BF16)),
        in_specs=[smem, vmem],
        out_specs=(vmem, vmem),
        compiler_params=pltpu.CompilerParams(vmem_limit_bytes=16 << 20),
    )(face_order, own)
    operand = pltpu.VMEM((2 * iface, 2 * width), BF16)
    out_shape = jax.ShapeDtypeStruct((face_blocks, 2, BLK, width), BF16)
    own_out, cross_out = pl.pallas_call(
        functools.partial(gather_kernel, n),
        out_shape=(out_shape, out_shape),
        in_specs=[vmem, vmem],
        out_specs=(vmem, vmem),
        scratch_shapes=[pltpu.VMEM((points, 2 * iface), BF16)] * 2
        + [pltpu.VMEM((2, 2 * iface, 2 * width), BF16)]
        + [operand] * 2
        + [buffer] * 4 + [pltpu.SemaphoreType.DMA((chunks,))] * 6,
        compiler_params=pltpu.CompilerParams(
            collective_id=0, has_side_effects=True, vmem_limit_bytes=36 << 20
        ),
    )(mine, rows_in)

    merged = pl.pallas_call(
        place_kernel,
        out_shape=jax.ShapeDtypeStruct((2, 2 * points, width), BF16),
        in_specs=[smem, vmem, vmem],
        out_specs=pl.BlockSpec(memory_space=pl.ANY),
        scratch_shapes=[pltpu.SemaphoreType.DMA((2 * face_blocks,))],
        compiler_params=pltpu.CompilerParams(vmem_limit_bytes=16 << 20),
    )(face_order, own_out, cross_out)
    return merged[:, None, None]


def solution(mesh):
    in_specs = (P(None, "box", None, None, "grp"), P())
    out_specs = P(None, "box", None, None, "grp")
    return jax.shard_map(shards, mesh=mesh, in_specs=in_specs, out_specs=out_specs, check_vma=False)
```
